512 devices in a mesh: tab: 128 (over z, y, x_hi), col: 4 (over x_lo, core).
Axes of the slice: x: 4 (x_hi: 2, x_lo: 2; x = x_hi * 2 + x_lo), y: 8, z: 8, core: 2. Of those that a mesh axis runs over, the one named last changes fastest.
Arguments:
- pooled: bfloat16 [4096, 128, 512], P('tab', None, 'col'), may hold values from -0.375 to 0.375
- pair_grads: bfloat16 [4096, 8128], P('tab', 'col'), may hold values from -6 to 6
- sample_slot: int32 [4096], replicated, may hold values from 0 to 4095, each once
- table_order: int32 [128], replicated, may hold values from 0 to 127, each once
Outputs:
- table_grads: bfloat16 [128, 4096, 512], P('tab', None, 'col')
The draws below stay inside these ranges and needn't reach their ends.
Inputs may be any that keep to these rules, and one draw needn't show every extreme that they name: Sample b sits at row sample_slot[b] of the arrays in owner order; every row holds one sample. Index k of tab owns table table_order[k]; each table once.
All inputs are finite; a program needn't handle non-finite values.
Results may differ from the reference program's by a relative error of at most 0.001.
Values may be sent and summed in bfloat16 or wider, within the bound.
A program may use at most 64 MiB of HBM per device.

```python
import jax
import jax.numpy as jnp
import numpy as np
from jax import lax

D = 512
B_DEV = 32
F = 128
P_SIZE = 8128
B = 4096
N_TAB = 128


def shard_levels(own_key, shape, shards, smallest, largest):
    loudness = 1.0
    for axis_at, shards_of in shards:
        heights = jax.random.uniform(jax.random.fold_in(jax.random.fold_in(own_key, 6), axis_at), (shards_of,), jnp.float32, smallest / len(shards), largest / len(shards))
        loudness = loudness * jnp.repeat(jnp.exp(heights), shape[axis_at] // shards_of).reshape((-1,) + (1,) * (len(shape) - 1 - axis_at))
    return loudness


def bell_draw(stream_key, extent, deviation, reach, pieces=(), held_as=jnp.bfloat16):
    entries = deviation * jax.random.normal(stream_key, extent, jnp.float32)
    if pieces:
        entries = entries * shard_levels(stream_key, extent, pieces, -0.22, 0.18)
    return jnp.clip(entries, -reach, reach).astype(held_as)


def setup_inputs(seed: int = 0) -> dict:
    splits = jax.random.split(jax.random.key(seed), 5)
    return {
        "pooled": bell_draw(splits[0], (B, F, D), 0.0625, 0.375, ((0, 128), (2, 4))),
        "pair_grads": bell_draw(splits[1], (B, P_SIZE), 1.0, 6.0, ((0, 128), (1, 4))),
        "sample_slot": jax.random.permutation(splits[2], B).astype(jnp.int32),
        "table_order": jax.random.permutation(splits[3], F).astype(jnp.int32),
    }


def pair_table(count):
    row_ids = np.arange(count)[:, None]
    col_ids = np.arange(count)[None, :]
    larger = np.maximum(row_ids, col_ids)
    smaller = np.minimum(row_ids, col_ids)
    table = larger * (larger - 1) // 2 + smaller
    table = np.where(row_ids == col_ids, count * (count - 1) // 2, table)
    return table.astype(np.int32)


def reference(pooled, pair_grads, sample_slot, table_order):
    table = jnp.asarray(pair_table(F))[table_order].reshape(-1).astype(jnp.int32)

    def one_owner(operands):
        grad_rows, emb_rows = operands
        padded = jnp.concatenate([grad_rows, jnp.zeros((grad_rows.shape[0], 1), jnp.bfloat16)], axis=1)
        tiles = jnp.take(padded, table, axis=1).reshape(-1, F, F)
        return jnp.einsum("bij,bjd->ibd", tiles.astype(jnp.float32), emb_rows.astype(jnp.float32)).astype(jnp.bfloat16)

    blocks = lax.map(one_owner, (pair_grads.reshape(N_TAB, B_DEV, P_SIZE), pooled.reshape(N_TAB, B_DEV, F, D)))
    owner_major = jnp.transpose(blocks, (1, 0, 2, 3)).reshape(F, B, D)
    return jnp.take(owner_major, sample_slot, axis=1)
```

```python
import functools

import jax
import jax.numpy as jnp
from jax import lax
from jax.experimental import pallas as pl
from jax.experimental.pallas import tpu as pltpu
from jax.sharding import PartitionSpec as P

MESH = pl.DeviceIdType.MESH
LANES = 128
SIGNALS_A_STEP = 8


def row_pieces(a, quarter):
    at, here, left, out = a * (a - 1) // 2, 0, a, []
    while left:
        part, local = at // quarter, at % quarter
        tile, lane = local // LANES, local % LANES
        count = min(left, quarter - local, LANES - lane)
        out.append((part, tile, lane, here, count))
        at, here, left = at + count, here + count, left - count
    return out


def exchange(tabs, cols, pooled, pairs_in, order, out, pairs, lower, grads, send, pair_send, pair_recv, row_send, row_recv):
    rows, tables, _ = pooled.shape
    quarter = pairs_in.shape[1]
    me, col = lax.axis_index("tab"), lax.axis_index("col")

    barrier = pltpu.get_barrier_semaphore()
    for k in range(1, cols):
        pl.semaphore_signal(barrier, inc=1, device_id={"col": (col + k) % cols}, device_id_type=MESH)

    def greet(i, carry):
        pl.semaphore_signal(barrier, inc=1, device_id={"tab": (me + i) % tabs}, device_id_type=MESH)
        return carry

    lax.fori_loop(1, tabs, greet, 0)
    pl.semaphore_wait(barrier, tabs + cols - 2)

    copies = []
    for k in range(1, cols):
        copy = pltpu.make_async_remote_copy(
            src_ref=pairs_in,
            dst_ref=pairs.at[col],
            send_sem=pair_send.at[k - 1],
            recv_sem=pair_recv.at[k - 1],
            device_id={"col": (col + k) % cols},
            device_id_type=MESH,
        )
        copy.start()
        copies.append(copy)
    pairs[col] = pairs_in[...]
    for copy in copies:
        copy.wait()

    lane = lax.broadcasted_iota(jnp.int32, (rows, LANES), 1)
    lower[pl.ds(0, rows, stride=tables), :] = jnp.zeros((rows, LANES), jnp.float32)
    for a in range(1, tables):
        row = jnp.zeros((rows, LANES), jnp.float32)
        for part, tile, there, here, count in row_pieces(a, quarter):
            width = min(LANES, quarter - tile * LANES)
            piece = pairs[part, :, tile * LANES : tile * LANES + width].astype(jnp.float32)
            if width < LANES:
                piece = jnp.concatenate([piece, jnp.zeros((rows, LANES - width), jnp.float32)], axis=1)
            shift = (here - there) % LANES
            if shift:
                piece = pltpu.roll(piece, shift, 1)
            row = jnp.where((lane >= here) & (lane < here + count), piece, row)
        lower[pl.ds(a, rows, stride=tables), :] = row

    flat = grads.reshape(tables * rows, LANES)

    def multiply(r, carry):
        half = lower[pl.ds(pl.multiple_of(r * tables, tables), tables), :]
        both = (half + half.T).astype(jnp.bfloat16)
        flat[pl.ds(r, tables, stride=rows), :] = jnp.dot(both, pooled[r], preferred_element_type=jnp.float32)
        return carry

    lax.fori_loop(0, rows, multiply, 0)

    def place(k, carry):
        send[k] = grads[order[k]].astype(jnp.bfloat16)
        return carry

    lax.fori_loop(0, tables, place, 0)

    def start(i, carry):
        to = (me + i * 45) % tabs
        pltpu.make_async_remote_copy(
            src_ref=send.at[to],
            dst_ref=out.at[me],
            send_sem=row_send,
            recv_sem=row_recv,
            device_id={"tab": to},
            device_id_type=MESH,
        ).start()
        return carry

    lax.fori_loop(1, tabs, start, 0)
    out[me] = send[me]
    others = out.at[pl.ds(0, tabs - 1)]
    pltpu.make_async_copy(others, others, row_recv).wait()
    sent = send.at[pl.ds(0, tabs - 1)]
    pltpu.make_async_copy(sent, sent, row_send).wait()


def reorder(slot, rows_in, out, wide, picked):
    wide[...] = rows_in[...].astype(jnp.float32)

    def step(i, carry):
        for u in range(16):
            b = i * 16 + u
            picked[pl.ds(b, 1), :] = wide[pl.ds(slot[b], 1), :]
        return carry

    lax.fori_loop(0, out.shape[0] // 16, step, 0)
    out[...] = picked[...].astype(out.dtype)


def per_device(tabs, cols, pooled, pair_grads, sample_slot, table_order):
    rows, tables, width = pooled.shape
    vmem = pl.BlockSpec(memory_space=pltpu.VMEM)
    smem = pl.BlockSpec(memory_space=pltpu.SMEM)
    received = pl.pallas_call(
        functools.partial(exchange, tabs, cols),
        out_shape=jax.ShapeDtypeStruct((tabs, rows, width), jnp.bfloat16),
        in_specs=[vmem, vmem, smem],
        out_specs=vmem,
        scratch_shapes=[
            pltpu.VMEM((cols,) + pair_grads.shape, jnp.bfloat16),
            pltpu.VMEM((rows * tables, LANES), jnp.float32),
            pltpu.VMEM((tables, rows, width), jnp.float32),
            pltpu.VMEM((tables, rows, width), jnp.bfloat16),
            pltpu.SemaphoreType.DMA((cols - 1,)),
            pltpu.SemaphoreType.DMA((cols - 1,)),
            pltpu.SemaphoreType.DMA,
            pltpu.SemaphoreType.DMA,
        ],
        compiler_params=pltpu.CompilerParams(collective_id=0, has_side_effects=True, vmem_limit_bytes=32 << 20),
        name="exchange",
    )(pooled, pair_grads, table_order)
    total = tabs * rows
    ordered = pl.pallas_call(
        reorder,
        out_shape=jax.ShapeDtypeStruct((total, width), jnp.bfloat16),
        in_specs=[smem, vmem],
        out_specs=vmem,
        scratch_shapes=[pltpu.VMEM((total, width), jnp.float32), pltpu.VMEM((total, width), jnp.float32)],
        compiler_params=pltpu.CompilerParams(vmem_limit_bytes=32 << 20),
        name="reorder",
    )(sample_slot, received.reshape(total, width))
    return ordered.reshape(1, total, width)


def solution(mesh):
    placed = (P("tab", None, "col"), P("tab", "col"), P(), P())
    return jax.shard_map(
        functools.partial(per_device, mesh.shape["tab"], mesh.shape["col"]),
        mesh=mesh,
        in_specs=placed,
        out_specs=P("tab", None, "col"),
        check_vma=False,
    )
```

```python
import functools

import jax
import jax.numpy as jnp
from jax import lax
from jax.experimental import pallas as pl
from jax.experimental.pallas import tpu as pltpu
from jax.sharding import PartitionSpec as P

MESH = pl.DeviceIdType.MESH
LANES = 128
PART = 16
SENDERS = 32
BLOCK = 1024
STRIDE = 77


def row_pieces(a, quarter):
    at, here, left, out = a * (a - 1) // 2, 0, a, []
    while left:
        part, local = at // quarter, at % quarter
        tile, lane = local // LANES, local % LANES
        count = min(left, quarter - local, LANES - lane)
        out.append((part, tile, lane, here, count))
        at, here, left = at + count, here + count, left - count
    return out


def by_distance():
    offsets = [(dz, dy, dx) for dz in range(8) for dy in range(8) for dx in range(2)][1:]
    return sorted(offsets, key=lambda o: -(min(o[0], 8 - o[0]) + min(o[1], 8 - o[1]) + 2 * o[2]))


def exchange(
    tabs, pooled_in, pairs_in, slot_in, order_in, out, pairs, pooled, slot, order, lower, grads, send, landed, wide, total,
    own_sem, pooled_sem, slot_sem, order_sem, pair_send, pair_recv, row_send, row_recv,
):
    rows, tables, _ = pooled.shape
    quarter = pairs.shape[2]
    parts = rows // PART
    me, col = lax.axis_index("tab"), lax.axis_index("col")
    sibling = col + 1 - 2 * (col % 2)
    across = (col + 2) % 4

    own = pltpu.make_async_copy(pairs_in, pairs.at[col], own_sem)
    get_pooled = pltpu.make_async_copy(pooled_in, pooled, pooled_sem)
    get_slot = pltpu.make_async_copy(slot_in, slot, slot_sem)
    get_order = pltpu.make_async_copy(order_in, order, order_sem)
    own.start()
    get_pooled.start()
    get_order.start()
    get_slot.start()

    barrier = pltpu.get_barrier_semaphore()
    for peer in (across, sibling):
        pl.semaphore_signal(barrier, inc=1, device_id={"col": peer}, device_id_type=MESH)
    z, y, x = me // 16, (me // 2) % 8, me % 2
    for dz, dy, dx in by_distance():
        to = ((z + dz) % 8) * 16 + ((y + dy) % 8) * 2 + (x + dx) % 2
        pl.semaphore_signal(barrier, inc=1, device_id={"tab": to}, device_id_type=MESH)
    own.wait()
    pl.semaphore_wait(barrier, tabs + 1)

    def pass_pairs(lane, part, slot, peer):
        copy = pltpu.make_async_remote_copy(
            src_ref=pairs.at[slot, pl.ds(part * PART, PART)],
            dst_ref=pairs.at[slot, pl.ds(part * PART, PART)],
            send_sem=pair_send.at[lane, part],
            recv_sem=pair_recv.at[lane, part],
            device_id={"col": peer},
            device_id_type=MESH,
        )
        copy.start()
        return copy

    direct = [pass_pairs(0, p, col, across) for p in range(parts)]
    beside = [pass_pairs(1, p, col, sibling) for p in range(parts)]
    passed = []
    direct[0].wait_recv()
    passed.append(pass_pairs(2, 0, across, sibling))

    lane = lax.broadcasted_iota(jnp.int32, (PART, LANES), 1)
    flat = grads.reshape(tables * rows, LANES)
    groups = tabs // SENDERS

    def rows_of(part, i):
        return landed.at[part * groups + i // SENDERS, pl.ds(pl.multiple_of((i % SENDERS) * PART, PART), PART)]

    def multiply(r, carry):
        half = lower[pl.ds(pl.multiple_of(r * tables, tables), tables), :]
        both = (half + half.T).astype(jnp.bfloat16)
        flat[pl.ds(r, tables, stride=rows), :] = jnp.dot(both, pooled[r], preferred_element_type=jnp.float32)
        return carry

    for part in range(parts):
        span = pl.ds(part * PART, PART)
        beside[part].wait_recv()
        passed[part].wait_recv()
        lower[pl.ds(part * PART * tables, PART, stride=tables), :] = jnp.zeros((PART, LANES), jnp.float32)
        for a in range(1, tables):
            row = jnp.zeros((PART, LANES), jnp.float32)
            for source, tile, there, first, count in row_pieces(a, quarter):
                width = min(LANES, quarter - tile * LANES)
                piece = pairs[source, span, tile * LANES : tile * LANES + width].astype(jnp.float32)
                if width < LANES:
                    piece = jnp.concatenate([piece, jnp.zeros((PART, LANES - width), jnp.float32)], axis=1)
                shift = (first - there) % LANES
                if shift:
                    piece = pltpu.roll(piece, shift, 1)
                row = jnp.where((lane >= first) & (lane < first + count), piece, row)
            lower[pl.ds(part * PART * tables + a, PART, stride=tables), :] = row
        if part + 1 < parts:
            direct[part + 1].wait_recv()
            passed.append(pass_pairs(2, part + 1, across, sibling))
        if part == 0:
            get_pooled.wait()
            get_order.wait()
        lax.fori_loop(part * PART, (part + 1) * PART, multiply, 0, unroll=8)

        def place(k, carry):
            send[k, span] = grads[order[k]][part * PART : (part + 1) * PART].astype(jnp.bfloat16)
            return carry

        lax.fori_loop(0, tables, place, 0, unroll=8)

        def start(i, carry):
            to = (me + i * STRIDE) % tabs
            pltpu.make_async_remote_copy(
                src_ref=send.at[to, span],
                dst_ref=rows_of(part, i),
                send_sem=row_send.at[part],
                recv_sem=row_recv.at[part * groups + i // SENDERS],
                device_id={"tab": to},
                device_id_type=MESH,
            ).start()
            return carry

        lax.fori_loop(1, tabs, start, 0)
        pltpu.make_async_copy(send.at[me, span], rows_of(part, 0), row_recv.at[part * groups]).start()

    get_slot.wait()
    for i in range(slot.shape[0]):
        wide[pl.ds(i * LANES, LANES), :] = jnp.broadcast_to(slot[pl.ds(i, 1), :], (LANES, LANES)).T
    total[...] = jnp.zeros_like(total)

    lane_id = lax.broadcasted_iota(jnp.int32, (1, LANES), 1)

    def add_group(g, carry):
        pltpu.make_async_copy(landed.at[g], landed.at[g], row_recv.at[g]).wait()
        first = (g % groups) * SENDERS
        held = landed[g]
        row_ids = []
        for t in range(SENDERS * PART // LANES):
            step = first + t * (LANES // PART) + lane_id // PART
            sender = (me - step * STRIDE + tabs * STRIDE) % tabs
            row_ids.append(sender * rows + (g // groups) * PART + lane_id % PART)

        def add(b, c):
            at = pl.ds(pl.multiple_of(b * BLOCK, BLOCK), BLOCK)
            wanted = wide[at, :]
            picks = jnp.concatenate(
                [jnp.where(wanted == ids, jnp.bfloat16(1), jnp.bfloat16(0)) for ids in row_ids], axis=1
            )
            total[at, :] += jnp.dot(picks, held, preferred_element_type=jnp.float32)
            return c

        lax.fori_loop(0, tabs * rows // BLOCK, add, 0, unroll=4)
        return carry

    lax.fori_loop(0, parts * groups, add_group, 0)
    out[...] = total[...].astype(out.dtype)

    for part in range(parts):
        direct[part].wait_send()
        beside[part].wait_send()
        passed[part].wait_send()
        sent = send.at[pl.ds(0, tabs - 1), pl.ds(part * PART, PART)]
        pltpu.make_async_copy(sent, sent, row_send.at[part]).wait()


def per_device(tabs, cols, pooled, pair_grads, sample_slot, table_order):
    rows, tables, width = pooled.shape
    vmem = pl.BlockSpec(memory_space=pltpu.VMEM)
    here = pl.BlockSpec(memory_space=pltpu.HBM)
    parts = rows // PART
    total = tabs * rows
    groups = parts * tabs // SENDERS
    ordered = pl.pallas_call(
        functools.partial(exchange, tabs),
        out_shape=jax.ShapeDtypeStruct((total, width), jnp.bfloat16),
        in_specs=[here] * 4,
        out_specs=vmem,
        scratch_shapes=[
            pltpu.VMEM((cols,) + pair_grads.shape, jnp.bfloat16),
            pltpu.VMEM(pooled.shape, jnp.bfloat16),
            pltpu.VMEM((total // LANES, LANES), jnp.int32),
            pltpu.SMEM((tables,), jnp.int32),
            pltpu.VMEM((rows * tables, LANES), jnp.float32),
            pltpu.VMEM((tables, rows, width), jnp.float32),
            pltpu.VMEM((tables, rows, width), jnp.bfloat16),
            pltpu.VMEM((groups, SENDERS * PART, width), jnp.bfloat16),
            pltpu.VMEM((total, LANES), jnp.int32),
            pltpu.VMEM((total, width), jnp.float32),
            pltpu.SemaphoreType.DMA,
            pltpu.SemaphoreType.DMA,
            pltpu.SemaphoreType.DMA,
            pltpu.SemaphoreType.DMA,
            pltpu.SemaphoreType.DMA((3, parts)),
            pltpu.SemaphoreType.DMA((3, parts)),
            pltpu.SemaphoreType.DMA((parts,)),
            pltpu.SemaphoreType.DMA((groups,)),
        ],
        compiler_params=pltpu.CompilerParams(collective_id=0, has_side_effects=True, vmem_limit_bytes=60 << 20),
        name="exchange",
    )(pooled, pair_grads, sample_slot.reshape(total // LANES, LANES), table_order)
    return ordered.reshape(1, total, width)


def solution(mesh):
    placed = (P("tab", None, "col"), P("tab", "col"), P(), P())
    return jax.shard_map(
        functools.partial(per_device, mesh.shape["tab"], mesh.shape["col"]),
        mesh=mesh,
        in_specs=placed,
        out_specs=P("tab", None, "col"),
        check_vma=False,
    )
```

```python
import functools

import jax
import jax.numpy as jnp
from jax import lax
from jax.experimental import pallas as pl
from jax.experimental.pallas import tpu as pltpu
from jax.sharding import PartitionSpec as P

MESH = pl.DeviceIdType.MESH
LANES = 128
PART = 16
PLANE = 16
BLOCK = 1024
SECOND = 4096
STRIDE = 77


def row_pieces(a, quarter):
    at, here, left, out = a * (a - 1) // 2, 0, a, []
    while left:
        part, local = at // quarter, at % quarter
        tile, lane = local // LANES, local % LANES
        count = min(left, quarter - local, LANES - lane)
        out.append((part, tile, lane, here, count))
        at, here, left = at + count, here + count, left - count
    return out


def exchange(
    tabs, pooled_in, pairs_in, slot_in, order_in, out, pairs, pooled, slot, order, lower, grads, send, landed, wide, total,
    own_sem, pooled_sem, slot_sem, order_sem, pair_send, pair_recv, row_send, row_recv, answers,
):
    rows, tables, _ = pooled.shape
    quarter = pairs.shape[2]
    parts = rows // PART
    me, col = lax.axis_index("tab"), lax.axis_index("col")
    plane = me // PLANE
    sibling = col + 1 - 2 * (col % 2)
    across = (col + 2) % 4

    own = pltpu.make_async_copy(pairs_in, pairs.at[col], own_sem)
    get_pooled = pltpu.make_async_copy(pooled_in, pooled, pooled_sem)
    get_slot = pltpu.make_async_copy(slot_in, slot, slot_sem)
    get_order = pltpu.make_async_copy(order_in, order, order_sem)
    own.start()
    get_pooled.start()
    get_order.start()
    get_slot.start()

    barrier = pltpu.get_barrier_semaphore()
    for peer in (across, sibling):
        pl.semaphore_signal(barrier, inc=1, device_id={"col": peer}, device_id_type=MESH)

    def signal_tab(sem, to):
        pl.semaphore_signal(sem, inc=1, device_id={"tab": to}, device_id_type=MESH)

    def signal_span(sem, first, last):
        low, high = (first + PLANE - 1) // PLANE, last // PLANE

        def one(to, carry):
            signal_tab(sem, to)
            return carry

        def block(p, carry):
            for k in range(PLANE):
                signal_tab(sem, p * PLANE + k)
            return carry

        lax.fori_loop(first, jnp.minimum(low * PLANE, last), one, 0)
        lax.fori_loop(low, high, block, 0)
        lax.fori_loop(jnp.maximum(high * PLANE, first), last, one, 0)

    signal_span(barrier, me + 1, tabs)
    own.wait()
    pl.semaphore_wait(barrier, me + 2)

    def pass_pairs(lane, part, slot, peer):
        copy = pltpu.make_async_remote_copy(
            src_ref=pairs.at[slot, pl.ds(part * PART, PART)],
            dst_ref=pairs.at[slot, pl.ds(part * PART, PART)],
            send_sem=pair_send.at[lane, part],
            recv_sem=pair_recv.at[lane, part],
            device_id={"col": peer},
            device_id_type=MESH,
        )
        copy.start()
        return copy

    direct = [pass_pairs(0, p, col, across) for p in range(parts)]
    beside = [pass_pairs(1, p, col, sibling) for p in range(parts)]

    signal_span(answers, 0, me)
    passed = []
    direct[0].wait_recv()
    passed.append(pass_pairs(2, 0, across, sibling))

    lane = lax.broadcasted_iota(jnp.int32, (PART, LANES), 1)
    flat = grads.reshape(tables * rows, LANES)
    planes = tabs // PLANE

    def multiply(r, carry):
        half = lower[pl.ds(pl.multiple_of(r * tables, tables), tables), :]
        both = (half + half.T).astype(jnp.bfloat16)
        flat[pl.ds(r, tables, stride=rows), :] = jnp.dot(both, pooled[r], preferred_element_type=jnp.float32)
        return carry

    for part in range(parts):
        span = pl.ds(part * PART, PART)
        beside[part].wait_recv()
        passed[part].wait_recv()
        lower[pl.ds(part * PART * tables, PART, stride=tables), :] = jnp.zeros((PART, LANES), jnp.float32)
        for a in range(1, tables):
            row = jnp.zeros((PART, LANES), jnp.float32)
            for source, tile, there, first, count in row_pieces(a, quarter):
                width = min(LANES, quarter - tile * LANES)
                piece = pairs[source, span, tile * LANES : tile * LANES + width].astype(jnp.float32)
                if width < LANES:
                    piece = jnp.concatenate([piece, jnp.zeros((PART, LANES - width), jnp.float32)], axis=1)
                shift = (first - there) % LANES
                if shift:
                    piece = pltpu.roll(piece, shift, 1)
                row = jnp.where((lane >= first) & (lane < first + count), piece, row)
            lower[pl.ds(part * PART * tables + a, PART, stride=tables), :] = row
        if part == 0:
            get_pooled.wait()
            get_order.wait()
        lax.fori_loop(part * PART, (part + 1) * PART, multiply, 0, unroll=8)

        def place(k, carry):
            send[k, span] = grads[order[k]][part * PART : (part + 1) * PART].astype(jnp.bfloat16)
            return carry

        lax.fori_loop(0, tables, place, 0, unroll=8)

        if part + 1 < parts:
            direct[part + 1].wait_recv()
            passed.append(pass_pairs(2, part + 1, across, sibling))
        if part == 0:

            @pl.when(me < tabs - 1)
            def _():
                pl.semaphore_wait(answers, tabs - 1 - me)


        def start(i, carry):
            to = (me + i * STRIDE) % tabs
            pltpu.make_async_remote_copy(
                src_ref=send.at[to, span],
                dst_ref=landed.at[part, me],
                send_sem=row_send.at[part],
                recv_sem=row_recv.at[part * planes + plane],
                device_id={"tab": to},
                device_id_type=MESH,
            ).start()
            return carry

        lax.fori_loop(1, tabs, start, 0)
        pltpu.make_async_copy(send.at[me, span], landed.at[part, me], row_recv.at[part * planes + plane]).start()

    get_slot.wait()
    at = slot[...]
    key = (at // PART % parts) * (tabs * PART // 2) + at // (2 * PLANE * rows) * (PLANE * PART)
    key += at // rows % PLANE * PART + at % PART
    slot[...] = key + at // (PLANE * rows) % 2 * SECOND
    for i in range(slot.shape[0]):
        wide[pl.ds(i * LANES, LANES), :] = jnp.broadcast_to(slot[pl.ds(i, 1), :], (LANES, LANES)).T
    total[...] = jnp.zeros_like(total)

    lane_id = lax.broadcasted_iota(jnp.int32, (1, LANES), 1)

    def add_group(g, carry):
        part, p = g // (planes // 2), g % (planes // 2) * 2
        held = []
        for q in range(2):
            at = pl.ds((p + q) * PLANE, PLANE)
            group = landed.at[part, at]
            pltpu.make_async_copy(group, group, row_recv.at[part * planes + p + q]).wait()
            held.append(landed[part, at].reshape(PLANE * PART, LANES))
        held = jnp.concatenate(held, axis=1)
        row_ids = [lane_id + (g * PLANE * PART + t * LANES) for t in range(PLANE * PART // LANES)]

        def add(b, c):
            at = pl.ds(pl.multiple_of(b * BLOCK, BLOCK), BLOCK)
            wanted = wide[at, :]
            second = wanted >= SECOND
            wanted = jnp.where(second, wanted - SECOND, wanted)
            picks = jnp.concatenate(
                [jnp.where(wanted == ids, jnp.bfloat16(1), jnp.bfloat16(0)) for ids in row_ids], axis=1
            )
            both = jnp.dot(picks, held, preferred_element_type=jnp.float32)
            total[at, :] += jnp.where(second, both[:, LANES:], both[:, :LANES])
            return c

        lax.fori_loop(0, tabs * rows // BLOCK, add, 0, unroll=4)
        return carry

    lax.fori_loop(0, parts * planes // 2, add_group, 0)
    out[...] = total[...].astype(out.dtype)

    for part in range(parts):
        direct[part].wait_send()
        beside[part].wait_send()
        passed[part].wait_send()
        sent = send.at[pl.ds(0, tabs - 1), pl.ds(part * PART, PART)]
        pltpu.make_async_copy(sent, sent, row_send.at[part]).wait()


def per_device(tabs, cols, pooled, pair_grads, sample_slot, table_order):
    rows, tables, width = pooled.shape
    vmem = pl.BlockSpec(memory_space=pltpu.VMEM)
    here = pl.BlockSpec(memory_space=pltpu.HBM)
    parts = rows // PART
    total = tabs * rows
    ordered = pl.pallas_call(
        functools.partial(exchange, tabs),
        out_shape=jax.ShapeDtypeStruct((total, width), jnp.bfloat16),
        in_specs=[here] * 4,
        out_specs=vmem,
        scratch_shapes=[
            pltpu.VMEM((cols,) + pair_grads.shape, jnp.bfloat16),
            pltpu.VMEM(pooled.shape, jnp.bfloat16),
            pltpu.VMEM((total // LANES, LANES), jnp.int32),
            pltpu.SMEM((tables,), jnp.int32),
            pltpu.VMEM((rows * tables, LANES), jnp.float32),
            pltpu.VMEM((tables, rows, width), jnp.float32),
            pltpu.VMEM((tables, rows, width), jnp.bfloat16),
            pltpu.VMEM((parts, tabs, PART, width), jnp.bfloat16),
            pltpu.VMEM((total, LANES), jnp.int32),
            pltpu.VMEM((total, width), jnp.float32),
            pltpu.SemaphoreType.DMA,
            pltpu.SemaphoreType.DMA,
            pltpu.SemaphoreType.DMA,
            pltpu.SemaphoreType.DMA,
            pltpu.SemaphoreType.DMA((3, parts)),
            pltpu.SemaphoreType.DMA((3, parts)),
            pltpu.SemaphoreType.DMA((parts,)),
            pltpu.SemaphoreType.DMA((parts * tabs // PLANE,)),
            pltpu.SemaphoreType.REGULAR,
        ],
        compiler_params=pltpu.CompilerParams(collective_id=0, has_side_effects=True, vmem_limit_bytes=60 << 20),
        name="exchange",
    )(pooled, pair_grads, sample_slot.reshape(total // LANES, LANES), table_order)
    return ordered.reshape(1, total, width)


def solution(mesh):
    placed = (P("tab", None, "col"), P("tab", "col"), P(), P())
    return jax.shard_map(
        functools.partial(per_device, mesh.shape["tab"], mesh.shape["col"]),
        mesh=mesh,
        in_specs=placed,
        out_specs=P("tab", None, "col"),
        check_vma=False,
    )
```

```python
import functools

import jax
import jax.numpy as jnp
from jax import lax
from jax.experimental import pallas as pl
from jax.experimental.pallas import tpu as pltpu
from jax.sharding import PartitionSpec as P

MESH = pl.DeviceIdType.MESH
LANES = 128
PART = 16
PLANE = 16
BLOCK = 1024
SECOND = 4096
STRIDE = 77


def row_pieces(a, quarter):
    at, here, left, out = a * (a - 1) // 2, 0, a, []
    while left:
        part, local = at // quarter, at % quarter
        tile, lane = local // LANES, local % LANES
        count = min(left, quarter - local, LANES - lane)
        out.append((part, tile, lane, here, count))
        at, here, left = at + count, here + count, left - count
    return out


def by_distance():
    groups = {}
    for dz in range(8):
        for dy in range(8):
            for dx in range(2):
                groups.setdefault((min(dz, 8 - dz), min(dy, 8 - dy), dx), []).append((dz, dy, dx))
    order = sorted(groups, key=lambda k: -sum(k))
    return [o for k in order for o in groups[k]][:-1]


def exchange(
    tabs, pooled_in, pairs_in, slot_in, order_in, out, pairs, pooled, slot, order, lower, grads, send, landed, wide, total,
    own_sem, pooled_sem, slot_sem, order_sem, pair_send, pair_recv, row_send, row_recv, answers,
):
    rows, tables, _ = pooled.shape
    quarter = pairs.shape[2]
    parts = rows // PART
    me, col = lax.axis_index("tab"), lax.axis_index("col")
    plane = me // PLANE
    z, y, x = me // 16, (me // 2) % 8, me % 2
    sibling = col + 1 - 2 * (col % 2)
    across = (col + 2) % 4

    own = pltpu.make_async_copy(pairs_in, pairs.at[col], own_sem)
    get_pooled = pltpu.make_async_copy(pooled_in, pooled, pooled_sem)
    get_slot = pltpu.make_async_copy(slot_in, slot, slot_sem)
    get_order = pltpu.make_async_copy(order_in, order, order_sem)
    own.start()
    get_pooled.start()
    get_order.start()
    get_slot.start()

    barrier = pltpu.get_barrier_semaphore()
    for peer in (across, sibling):
        pl.semaphore_signal(barrier, inc=1, device_id={"col": peer}, device_id_type=MESH)

    def signal_tab(sem, to):
        pl.semaphore_signal(sem, inc=1, device_id={"tab": to}, device_id_type=MESH)

    def signal_span(sem, first, last):
        low, high = (first + PLANE - 1) // PLANE, last // PLANE

        def one(to, carry):
            signal_tab(sem, to)
            return carry

        def block(p, carry):
            for k in range(PLANE):
                signal_tab(sem, p * PLANE + k)
            return carry

        lax.fori_loop(first, jnp.minimum(low * PLANE, last), one, 0)
        lax.fori_loop(low, high, block, 0)
        lax.fori_loop(jnp.maximum(high * PLANE, first), last, one, 0)

    signal_span(barrier, me + 1, tabs)
    own.wait()
    pl.semaphore_wait(barrier, me + 2)

    def pass_pairs(lane, part, slot, peer):
        copy = pltpu.make_async_remote_copy(
            src_ref=pairs.at[slot, pl.ds(part * PART, PART)],
            dst_ref=pairs.at[slot, pl.ds(part * PART, PART)],
            send_sem=pair_send.at[lane, part],
            recv_sem=pair_recv.at[lane, part],
            device_id={"col": peer},
            device_id_type=MESH,
        )
        copy.start()
        return copy

    direct = [pass_pairs(0, p, col, across) for p in range(parts)]
    beside = [pass_pairs(1, p, col, sibling) for p in range(parts)]

    signal_span(answers, 0, me)
    passed = []
    direct[0].wait_recv()
    passed.append(pass_pairs(2, 0, across, sibling))

    lane = lax.broadcasted_iota(jnp.int32, (PART, LANES), 1)
    flat = grads.reshape(tables * rows, LANES)
    planes = tabs // PLANE

    def multiply(r, carry):
        half = lower[pl.ds(pl.multiple_of(r * tables, tables), tables), :]
        both = (half + half.T).astype(jnp.bfloat16)
        flat[pl.ds(r, tables, stride=rows), :] = jnp.dot(both, pooled[r], preferred_element_type=jnp.float32)
        return carry

    for part in range(parts):
        span = pl.ds(part * PART, PART)
        beside[part].wait_recv()
        passed[part].wait_recv()
        lower[pl.ds(part * PART * tables, PART, stride=tables), :] = jnp.zeros((PART, LANES), jnp.float32)
        for a in range(1, tables):
            row = jnp.zeros((PART, LANES), jnp.float32)
            for source, tile, there, first, count in row_pieces(a, quarter):
                width = min(LANES, quarter - tile * LANES)
                piece = pairs[source, span, tile * LANES : tile * LANES + width].astype(jnp.float32)
                if width < LANES:
                    piece = jnp.concatenate([piece, jnp.zeros((PART, LANES - width), jnp.float32)], axis=1)
                shift = (first - there) % LANES
                if shift:
                    piece = pltpu.roll(piece, shift, 1)
                row = jnp.where((lane >= first) & (lane < first + count), piece, row)
            lower[pl.ds(part * PART * tables + a, PART, stride=tables), :] = row
        if part == 0:
            get_pooled.wait()
            get_order.wait()
        lax.fori_loop(part * PART, (part + 1) * PART, multiply, 0, unroll=8)

        def place(k, carry):
            send[k, span] = grads[order[k]][part * PART : (part + 1) * PART].astype(jnp.bfloat16)
            return carry

        lax.fori_loop(0, tables, place, 0, unroll=8)

        if part + 1 < parts:
            direct[part + 1].wait_recv()
            passed.append(pass_pairs(2, part + 1, across, sibling))
        if part == 0:

            @pl.when(me < tabs - 1)
            def _():
                pl.semaphore_wait(answers, tabs - 1 - me)


        for dz, dy, dx in by_distance():
            to = ((z + dz) % 8) * 16 + ((y + dy) % 8) * 2 + (x + dx) % 2
            pltpu.make_async_remote_copy(
                src_ref=send.at[to, span],
                dst_ref=landed.at[part, me],
                send_sem=row_send.at[part],
                recv_sem=row_recv.at[part * planes + plane],
                device_id={"tab": to},
                device_id_type=MESH,
            ).start()
        pltpu.make_async_copy(send.at[me, span], landed.at[part, me], row_recv.at[part * planes + plane]).start()

    get_slot.wait()
    at = slot[...]
    key = (at // PART % parts) * (tabs * PART // 2) + at // (2 * PLANE * rows) * (PLANE * PART)
    key += at // rows % PLANE * PART + at % PART
    slot[...] = key + at // (PLANE * rows) % 2 * SECOND
    for i in range(slot.shape[0]):
        wide[pl.ds(i * LANES, LANES), :] = jnp.broadcast_to(slot[pl.ds(i, 1), :], (LANES, LANES)).T
    total[...] = jnp.zeros_like(total)

    lane_id = lax.broadcasted_iota(jnp.int32, (1, LANES), 1)

    def add_group(g, carry):
        part, p = g // (planes // 2), g % (planes // 2) * 2
        held = []
        for q in range(2):
            at = pl.ds((p + q) * PLANE, PLANE)
            group = landed.at[part, at]
            pltpu.make_async_copy(group, group, row_recv.at[part * planes + p + q]).wait()
            held.append(landed[part, at].reshape(PLANE * PART, LANES))
        held = jnp.concatenate(held, axis=1)
        row_ids = [lane_id + (g * PLANE * PART + t * LANES) for t in range(PLANE * PART // LANES)]

        def add(b, c):
            at = pl.ds(pl.multiple_of(b * BLOCK, BLOCK), BLOCK)
            wanted = wide[at, :]
            second = wanted >= SECOND
            wanted = jnp.where(second, wanted - SECOND, wanted)
            picks = jnp.concatenate(
                [jnp.where(wanted == ids, jnp.bfloat16(1), jnp.bfloat16(0)) for ids in row_ids], axis=1
            )
            both = jnp.dot(picks, held, preferred_element_type=jnp.float32)
            total[at, :] += jnp.where(second, both[:, LANES:], both[:, :LANES])
            return c

        lax.fori_loop(0, tabs * rows // BLOCK, add, 0, unroll=4)
        return carry

    lax.fori_loop(0, parts * planes // 2, add_group, 0)
    out[...] = total[...].astype(out.dtype)

    for part in range(parts):
        direct[part].wait_send()
        beside[part].wait_send()
        passed[part].wait_send()
        sent = send.at[pl.ds(0, tabs - 1), pl.ds(part * PART, PART)]
        pltpu.make_async_copy(sent, sent, row_send.at[part]).wait()


def per_device(tabs, cols, pooled, pair_grads, sample_slot, table_order):
    rows, tables, width = pooled.shape
    vmem = pl.BlockSpec(memory_space=pltpu.VMEM)
    here = pl.BlockSpec(memory_space=pltpu.HBM)
    parts = rows // PART
    total = tabs * rows
    ordered = pl.pallas_call(
        functools.partial(exchange, tabs),
        out_shape=jax.ShapeDtypeStruct((total, width), jnp.bfloat16),
        in_specs=[here] * 4,
        out_specs=vmem,
        scratch_shapes=[
            pltpu.VMEM((cols,) + pair_grads.shape, jnp.bfloat16),
            pltpu.VMEM(pooled.shape, jnp.bfloat16),
            pltpu.VMEM((total // LANES, LANES), jnp.int32),
            pltpu.SMEM((tables,), jnp.int32),
            pltpu.VMEM((rows * tables, LANES), jnp.float32),
            pltpu.VMEM((tables, rows, width), jnp.float32),
            pltpu.VMEM((tables, rows, width), jnp.bfloat16),
            pltpu.VMEM((parts, tabs, PART, width), jnp.bfloat16),
            pltpu.VMEM((total, LANES), jnp.int32),
            pltpu.VMEM((total, width), jnp.float32),
            pltpu.SemaphoreType.DMA,
            pltpu.SemaphoreType.DMA,
            pltpu.SemaphoreType.DMA,
            pltpu.SemaphoreType.DMA,
            pltpu.SemaphoreType.DMA((3, parts)),
            pltpu.SemaphoreType.DMA((3, parts)),
            pltpu.SemaphoreType.DMA((parts,)),
            pltpu.SemaphoreType.DMA((parts * tabs // PLANE,)),
            pltpu.SemaphoreType.REGULAR,
        ],
        compiler_params=pltpu.CompilerParams(collective_id=0, has_side_effects=True, vmem_limit_bytes=60 << 20),
        name="exchange",
    )(pooled, pair_grads, sample_slot.reshape(total // LANES, LANES), table_order)
    return ordered.reshape(1, total, width)


def solution(mesh):
    placed = (P("tab", None, "col"), P("tab", "col"), P(), P())
    return jax.shard_map(
        functools.partial(per_device, mesh.shape["tab"], mesh.shape["col"]),
        mesh=mesh,
        in_specs=placed,
        out_specs=P("tab", None, "col"),
        check_vma=False,
    )
```

```python
import functools

import jax
import jax.numpy as jnp
from jax import lax
from jax.experimental import pallas as pl
from jax.experimental.pallas import tpu as pltpu
from jax.sharding import PartitionSpec as P

MESH = pl.DeviceIdType.MESH
LANES = 128
PART = 16
PLANE = 16
BLOCK = 1024
STRIDE = 77


def row_pieces(a, quarter):
    at, here, left, out = a * (a - 1) // 2, 0, a, []
    while left:
        part, local = at // quarter, at % quarter
        tile, lane = local // LANES, local % LANES
        count = min(left, quarter - local, LANES - lane)
        out.append((part, tile, lane, here, count))
        at, here, left = at + count, here + count, left - count
    return out


def by_distance():
    groups = {}
    for dz in range(8):
        for dy in range(8):
            for dx in range(2):
                groups.setdefault((min(dz, 8 - dz), min(dy, 8 - dy), dx), []).append((dz, dy, dx))
    order = sorted(groups, key=lambda k: -sum(k))
    return [o for k in order for o in groups[k]][:-1]


def exchange(
    tabs, pooled_in, pairs_in, slot_in, order_in, out, pairs, pooled, slot, order, lower, grads, send, landed, wide, side, total,
    own_sem, pooled_sem, slot_sem, order_sem, pair_send, pair_recv, row_send, row_recv, answers,
):
    rows, tables, _ = pooled.shape
    quarter = pairs.shape[2]
    parts = rows // PART
    me, col = lax.axis_index("tab"), lax.axis_index("col")
    plane = me // PLANE
    z, y, x = me // 16, (me // 2) % 8, me % 2
    sibling = col + 1 - 2 * (col % 2)
    across = (col + 2) % 4

    own = pltpu.make_async_copy(pairs_in, pairs.at[col], own_sem)
    get_pooled = pltpu.make_async_copy(pooled_in, pooled, pooled_sem)
    get_slot = pltpu.make_async_copy(slot_in, slot, slot_sem)
    get_order = pltpu.make_async_copy(order_in, order, order_sem)
    own.start()
    get_pooled.start()
    get_order.start()
    get_slot.start()

    barrier = pltpu.get_barrier_semaphore()
    for peer in (across, sibling):
        pl.semaphore_signal(barrier, inc=1, device_id={"col": peer}, device_id_type=MESH)

    def signal_tab(sem, to):
        pl.semaphore_signal(sem, inc=1, device_id={"tab": to}, device_id_type=MESH)

    def signal_span(sem, first, last):
        low, high = (first + PLANE - 1) // PLANE, last // PLANE

        def one(to, carry):
            signal_tab(sem, to)
            return carry

        def block(p, carry):
            for k in range(PLANE):
                signal_tab(sem, p * PLANE + k)
            return carry

        lax.fori_loop(first, jnp.minimum(low * PLANE, last), one, 0)
        lax.fori_loop(low, high, block, 0)
        lax.fori_loop(jnp.maximum(high * PLANE, first), last, one, 0)

    signal_span(barrier, me + 1, tabs)
    own.wait()
    pl.semaphore_wait(barrier, me + 2)

    def pass_pairs(lane, part, slot, peer):
        copy = pltpu.make_async_remote_copy(
            src_ref=pairs.at[slot, pl.ds(part * PART, PART)],
            dst_ref=pairs.at[slot, pl.ds(part * PART, PART)],
            send_sem=pair_send.at[lane, part],
            recv_sem=pair_recv.at[lane, part],
            device_id={"col": peer},
            device_id_type=MESH,
        )
        copy.start()
        return copy

    direct = [pass_pairs(0, p, col, across) for p in range(parts)]
    beside = [pass_pairs(1, p, col, sibling) for p in range(parts)]

    signal_span(answers, 0, me)
    passed = []
    direct[0].wait_recv()
    passed.append(pass_pairs(2, 0, across, sibling))

    lane = lax.broadcasted_iota(jnp.int32, (PART, LANES), 1)
    flat = grads.reshape(tables * rows, LANES)
    planes = tabs // PLANE

    def multiply(r, carry):
        half = lower[pl.ds(pl.multiple_of(r * tables, tables), tables), :]
        both = (half + half.T).astype(jnp.bfloat16)
        flat[pl.ds(r, tables, stride=rows), :] = jnp.dot(both, pooled[r], preferred_element_type=jnp.float32)
        return carry

    for part in range(parts):
        span = pl.ds(part * PART, PART)
        beside[part].wait_recv()
        passed[part].wait_recv()
        lower[pl.ds(part * PART * tables, PART, stride=tables), :] = jnp.zeros((PART, LANES), jnp.float32)
        for a in range(1, tables):
            row = jnp.zeros((PART, LANES), jnp.float32)
            for source, tile, there, first, count in row_pieces(a, quarter):
                width = min(LANES, quarter - tile * LANES)
                piece = pairs[source, span, tile * LANES : tile * LANES + width].astype(jnp.float32)
                if width < LANES:
                    piece = jnp.concatenate([piece, jnp.zeros((PART, LANES - width), jnp.float32)], axis=1)
                shift = (first - there) % LANES
                if shift:
                    piece = pltpu.roll(piece, shift, 1)
                row = jnp.where((lane >= first) & (lane < first + count), piece, row)
            lower[pl.ds(part * PART * tables + a, PART, stride=tables), :] = row
        if part == 0:
            get_pooled.wait()
            get_order.wait()
        lax.fori_loop(part * PART, (part + 1) * PART, multiply, 0, unroll=16)

        def place(k, carry):
            send[k, span] = grads[order[k]][part * PART : (part + 1) * PART].astype(jnp.bfloat16)
            return carry

        lax.fori_loop(0, tables, place, 0, unroll=16)

        if part == 0:

            @pl.when(me < tabs - 1)
            def _():
                pl.semaphore_wait(answers, tabs - 1 - me)


        for dz, dy, dx in by_distance():
            to = ((z + dz) % 8) * 16 + ((y + dy) % 8) * 2 + (x + dx) % 2
            pltpu.make_async_remote_copy(
                src_ref=send.at[to, span],
                dst_ref=landed.at[part, me],
                send_sem=row_send.at[part],
                recv_sem=row_recv.at[part * planes + plane],
                device_id={"tab": to},
                device_id_type=MESH,
            ).start()
        if part + 1 < parts:
            direct[part + 1].wait_recv()
            passed.append(pass_pairs(2, part + 1, across, sibling))
        pltpu.make_async_copy(send.at[me, span], landed.at[part, me], row_recv.at[part * planes + plane]).start()

    get_slot.wait()
    at = slot[...]
    key = (at // PART % parts) * (tabs * PART // 2) + at // (2 * PLANE * rows) * (PLANE * PART)
    key += at // rows % PLANE * PART + at % PART
    slot[...] = key
    half = at // (PLANE * rows) % 2
    for i in range(slot.shape[0]):
        wide[pl.ds(i * LANES, LANES), :] = jnp.broadcast_to(slot[pl.ds(i, 1), :], (LANES, LANES)).T
        side[pl.ds(i * LANES, LANES), :] = jnp.broadcast_to(half[i : i + 1, :], (LANES, LANES)).T
    total[...] = jnp.zeros_like(total)

    lane_id = lax.broadcasted_iota(jnp.int32, (1, LANES), 1)

    def add_group(g, carry):
        part, p = g // (planes // 2), g % (planes // 2) * 2
        held = []
        for q in range(2):
            at = pl.ds((p + q) * PLANE, PLANE)
            group = landed.at[part, at]
            pltpu.make_async_copy(group, group, row_recv.at[part * planes + p + q]).wait()
            held.append(landed[part, at].reshape(PLANE * PART, LANES))
        held = jnp.concatenate(held, axis=1)
        row_ids = [lane_id + (g * PLANE * PART + t * LANES) for t in range(PLANE * PART // LANES)]

        def add(b, c):
            at = pl.ds(pl.multiple_of(b * BLOCK, BLOCK), BLOCK)
            wanted = wide[at, :]
            picks = jnp.concatenate(
                [jnp.where(wanted == ids, jnp.bfloat16(1), jnp.bfloat16(0)) for ids in row_ids], axis=1
            )
            both = jnp.dot(picks, held, preferred_element_type=jnp.float32)
            total[at, :] += jnp.where(side[at, :] > 0, both[:, LANES:], both[:, :LANES])
            return c

        lax.fori_loop(0, tabs * rows // BLOCK, add, 0, unroll=4)
        return carry

    lax.fori_loop(0, parts * planes // 2, add_group, 0)
    out[...] = total[...].astype(out.dtype)

    for part in range(parts):
        direct[part].wait_send()
        beside[part].wait_send()
        passed[part].wait_send()
        sent = send.at[pl.ds(0, tabs - 1), pl.ds(part * PART, PART)]
        pltpu.make_async_copy(sent, sent, row_send.at[part]).wait()


def per_device(tabs, cols, pooled, pair_grads, sample_slot, table_order):
    rows, tables, width = pooled.shape
    vmem = pl.BlockSpec(memory_space=pltpu.VMEM)
    here = pl.BlockSpec(memory_space=pltpu.HBM)
    parts = rows // PART
    total = tabs * rows
    ordered = pl.pallas_call(
        functools.partial(exchange, tabs),
        out_shape=jax.ShapeDtypeStruct((total, width), jnp.bfloat16),
        in_specs=[here] * 4,
        out_specs=vmem,
        scratch_shapes=[
            pltpu.VMEM((cols,) + pair_grads.shape, jnp.bfloat16),
            pltpu.VMEM(pooled.shape, jnp.bfloat16),
            pltpu.VMEM((total // LANES, LANES), jnp.int32),
            pltpu.SMEM((tables,), jnp.int32),
            pltpu.VMEM((rows * tables, LANES), jnp.float32),
            pltpu.VMEM((tables, rows, width), jnp.float32),
            pltpu.VMEM((tables, rows, width), jnp.bfloat16),
            pltpu.VMEM((parts, tabs, PART, width), jnp.bfloat16),
            pltpu.VMEM((total, LANES), jnp.int32),
            pltpu.VMEM((total, LANES), jnp.int32),
            pltpu.VMEM((total, width), jnp.float32),
            pltpu.SemaphoreType.DMA,
            pltpu.SemaphoreType.DMA,
            pltpu.SemaphoreType.DMA,
            pltpu.SemaphoreType.DMA,
            pltpu.SemaphoreType.DMA((3, parts)),
            pltpu.SemaphoreType.DMA((3, parts)),
            pltpu.SemaphoreType.DMA((parts,)),
            pltpu.SemaphoreType.DMA((parts * tabs // PLANE,)),
            pltpu.SemaphoreType.REGULAR,
        ],
        compiler_params=pltpu.CompilerParams(collective_id=0, has_side_effects=True, vmem_limit_bytes=60 << 20),
        name="exchange",
    )(pooled, pair_grads, sample_slot.reshape(total // LANES, LANES), table_order)
    return ordered.reshape(1, total, width)


def solution(mesh):
    placed = (P("tab", None, "col"), P("tab", "col"), P(), P())
    return jax.shard_map(
        functools.partial(per_device, mesh.shape["tab"], mesh.shape["col"]),
        mesh=mesh,
        in_specs=placed,
        out_specs=P("tab", None, "col"),
        check_vma=False,
    )
```
